256 devices in a mesh: row: 32 (over y, z), col: 8 (over x, core).
Axes of the slice: x: 4, y: 4, z: 8, core: 2. Of those that a mesh axis runs over, the one named last changes fastest.
Arguments:
- kernel_configs: float32 [8, 2048, 16384], P(None, 'row', 'col'), may hold values from -1 to 2, as said below
- epoch_kernel: float32 [256, 256], replicated, may hold values from -1 to 2, as said below
- lengths: int32 [16384], P(('col', 'row')), may hold values from 1 to 256
- noise: float32 [16384], P(('col', 'row')), may hold values from 0.1 to 1
- curves: float32 [16384, 256], P(('col', 'row')), may hold values from -33 to 33
Outputs:
- solution: float32 [16384, 256], P(('col', 'row'))
- residual: float32 [16384, 256], P(('col', 'row'))
The draws below stay inside these ranges and needn't reach their ends.
Inputs may be any that keep to these rules, and one draw needn't show every extreme that they name: `kernel_configs`: reshaped to 16384 x 16384 by merging the first two dimensions, the matrix is symmetric positive definite. `epoch_kernel`: symmetric positive definite.
All inputs are finite; a program needn't handle non-finite values.
Results may differ from the reference program's by a relative error of at most 0.00026.
Values sent between devices are 32-bit elements; how exact they have to be, the bound alone decides.
No kernel may reach another device: no remote copies, remote signals or barrier semaphores. Data moves between devices by JAX's collectives and lax.ppermute only.
A program may use at most 64 MiB of HBM per device.

```python
import math
import jax
import jax.numpy as jnp
from jax import lax

E = 256
ITERS = 2
N = 16384
COLBLK = 2048
NCB = 8


def symmetric_draw(key, order):
    values = jax.random.normal(key, (order, order), jnp.float32)
    spread = 0.4 / math.sqrt(2.0 * order)
    return jnp.eye(order, dtype=jnp.float32) + spread * (values + values.T)


def draw_kernel_configs(key, part):
    full_matrix = symmetric_draw(jax.random.fold_in(key, 11), N)
    return full_matrix.reshape(NCB, COLBLK, N)


def draw_epoch_kernel(key, part):
    return symmetric_draw(jax.random.fold_in(key, 13), E)


def draw_lengths(key, part):
    first_key, second_key = jax.random.split(jax.random.fold_in(key, 17))
    tier = jax.random.randint(first_key, (N,), 0, 16)
    shift = (tier >= 8).astype(jnp.int32) + (tier >= 12).astype(jnp.int32) + (tier >= 14).astype(jnp.int32) + (tier >= 15).astype(jnp.int32)
    top_length = jnp.right_shift(jnp.full((N,), E, jnp.int32), shift)
    dropped = jax.random.randint(second_key, (N,), 0, jnp.maximum(top_length // 2, 1))
    return (top_length - dropped).at[0].set(E).astype(jnp.int32)


def draw_curves(key, part):
    first_key, second_key = jax.random.split(jax.random.fold_in(key, 19))
    base_values = jax.random.truncated_normal(first_key, -6.0, 6.0, (N, E), jnp.float32)
    level = jax.random.uniform(second_key, (N, 1), jnp.float32)
    position = jnp.arange(N, dtype=jnp.float32)[:, None] / N
    row_scale = jnp.power(10.0, level - 0.5) * jnp.power(3.0, position - 0.5)
    return base_values * row_scale


def block_scale(own_key, dims, cuts, smallest, top_value):
    def one(dim, blocks):
        steps = jax.random.uniform(jax.random.fold_in(jax.random.fold_in(own_key, 6), dim), (blocks,), jnp.float32, smallest / len(cuts), top_value / len(cuts))
        return jnp.repeat(jnp.exp(steps), dims[dim] // blocks).reshape((-1,) + (1,) * (len(dims) - dim - 1))

    gain = one(*cuts[0])
    for cut in cuts[1:]:
        gain = gain * one(*cut)
    return gain


def setup_inputs(seed: int = 0) -> dict:
    splits = jax.random.split(jax.random.key(seed), 6)
    return {
        "kernel_configs": draw_kernel_configs(jax.random.fold_in(splits[5], 71), 0),
        "epoch_kernel": draw_epoch_kernel(jax.random.fold_in(splits[5], 71), 0),
        "lengths": draw_lengths(jax.random.fold_in(splits[5], 71), 0),
        "noise": jnp.clip(jnp.exp(math.log(1.0) - 2.3025851 * jax.random.uniform(splits[3], (N,), jnp.float32) ** block_scale(splits[3], (N,), ((0, 256),), -0.2, 0.2)), 0.1, 1.0),
        "curves": draw_curves(jax.random.fold_in(splits[5], 71), 0),
    }


def apply_operator(vector, kernel_full, epoch_kernel, curve_mask, noise):
    masked = vector * curve_mask
    summed = jnp.dot(kernel_full, masked, precision=lax.Precision.HIGHEST, preferred_element_type=jnp.float32)
    smoothed = jnp.dot(summed, epoch_kernel, precision=lax.Precision.HIGHEST, preferred_element_type=jnp.float32)
    return curve_mask * smoothed + noise[:, None] * vector


def reference(kernel_configs, epoch_kernel, lengths, noise, curves):
    kernel_full = kernel_configs.reshape(N, N)
    epoch_index = jnp.arange(E, dtype=jnp.int32)
    curve_mask = (epoch_index[None, :] < lengths[:, None]).astype(jnp.float32)
    solution = jnp.zeros_like(curves)
    residual = curves * curve_mask
    direction = residual
    norm_now = jnp.sum(residual * residual)
    for iteration in range(ITERS):
        applied = apply_operator(direction, kernel_full, epoch_kernel, curve_mask, noise)
        step_size = norm_now / jnp.sum(direction * applied)
        solution = solution + step_size * direction
        residual = residual - step_size * applied
        norm_next = jnp.sum(residual * residual)
        direction = residual + (norm_next / norm_now) * direction
        norm_now = norm_next
    return solution, residual
```

```python
import jax
import jax.numpy as jnp
from jax import lax
from jax.experimental import pallas as pl
from jax.experimental.pallas import tpu as pltpu
from jax.sharding import PartitionSpec as P

NY, NZ, NX = 4, 8, 4
BLOCK = 64
EPOCHS = 256
F32 = jnp.float32
BF16 = jnp.bfloat16


def class_member(k, j):
    kh, kl, jh, jl = k // 2, k % 2, j // 4, j % 4
    return (kl + 2 * jh) * NZ + 2 * jl + (kh + jh) % 2


CLASSES = [[class_member(k, j) for j in range(8)] for k in range(4)]


def shift_y(d):
    return [(y * NZ + z, ((y + d) % NY) * NZ + z) for y in range(NY) for z in range(NZ)]


def shift_z(d):
    return [(y * NZ + z, y * NZ + (z + d) % NZ) for y in range(NY) for z in range(NZ)]


def shift_x(d):
    return [(x * 2 + c, ((x + d) % NX) * 2 + c) for x in range(NX) for c in range(2)]


SIBLING = [(c, c ^ 1) for c in range(8)]


def split(value):
    high = lax.reduce_precision(value, 8, 7)
    return high.astype(BF16), (value - high).astype(BF16)


def gather_row(block):
    copies = jnp.broadcast_to(block[None], (8, BLOCK, EPOCHS))
    own = lax.all_to_all(copies, "row", 0, 0, axis_index_groups=CLASSES)
    next_y = lax.ppermute(own, "row", shift_y(-1))
    last_y = lax.ppermute(own, "row", shift_y(1))
    next_z = lax.ppermute(own[:4], "row", shift_z(-1))
    last_z = lax.ppermute(own[4:], "row", shift_z(1))
    return own, next_y, next_z, last_z, last_y


def product_kernel(place, own, next_y, next_z, last_z, last_y, k_high, k_low, keep, send, high, low):
    colour, x, core = place[0], place[1], place[2]

    def put(ref, slot, first):
        k = lax.rem(colour + slot, 4)
        kh, kl = k // 2, lax.rem(k, 2)
        for j in range(ref.shape[0]):
            jh, jl = (j + first) // 4, (j + first) % 4
            row = (kl + 2 * jh) * NZ + 2 * jl + lax.rem(kh + jh, 2)
            at = pl.ds(pl.multiple_of(row * BLOCK, BLOCK), BLOCK)
            value = ref[j]
            top = value.astype(BF16)
            high[at, :] = top
            low[at, :] = (value - top.astype(F32)).astype(BF16)

    put(own, 0, 0)
    put(next_y, 1, 0)
    put(next_z, 2, 0)
    put(last_z, 2, 4)
    put(last_y, 3, 0)
    for b in range(8):
        rows = pl.ds(b * BLOCK, BLOCK)
        part = jnp.dot(k_high[rows, :], high[...], preferred_element_type=F32)
        part += jnp.dot(k_high[rows, :], low[...], preferred_element_type=F32)
        part += jnp.dot(k_low[rows, :], high[...], preferred_element_type=F32)
        dx = lax.rem(b // 2 - x + NX, NX)

        @pl.when(core == b % 2)
        def _():
            keep[dx] = part

        @pl.when(core != b % 2)
        def _():
            send[dx] = part


def product(place, parts, k_high, k_low):
    vmem = pl.BlockSpec(memory_space=pltpu.VMEM)
    half = jax.ShapeDtypeStruct((NX, BLOCK, EPOCHS), F32)
    return pl.pallas_call(
        product_kernel,
        out_shape=(half, half),
        in_specs=[pl.BlockSpec(memory_space=pltpu.SMEM)] + [vmem] * 7,
        out_specs=(vmem, vmem),
        scratch_shapes=[pltpu.VMEM((2048, EPOCHS), BF16), pltpu.VMEM((2048, EPOCHS), BF16)],
        compiler_params=pltpu.CompilerParams(vmem_limit_bytes=24 * 1024 * 1024),
        cost_estimate=pl.CostEstimate(
            flops=2 * 3 * 512 * 2048 * EPOCHS, bytes_accessed=7 * 1024 * 1024, transcendentals=0
        ),
    )(place, *parts, k_high, k_low)


def scatter_col(keep, send):
    total = keep + lax.ppermute(send, "col", SIBLING)
    got = [lax.ppermute(total[d], "col", shift_x(d)) for d in range(1, NX)]
    return total[0] + got[0] + got[1] + got[2]


def reduce_all(values):
    tile = jnp.zeros((8, 128), F32)
    lane = lax.broadcasted_iota(jnp.int32, (8, 128), 1)
    for i, v in enumerate(values):
        tile = jnp.where(lane == i, v, tile)
    tile = tile + lax.ppermute(tile, "col", SIBLING)
    tile = tile + sum(lax.ppermute(tile, "col", shift_x(d)) for d in range(1, NX))
    copies = jnp.broadcast_to(tile[None], (32, 8, 128))
    tile = jnp.sum(lax.all_to_all(copies, "row", 0, 0), axis=0)
    return [tile[0, i] for i in range(len(values))]


def per_device(kernel_configs, epoch_kernel, lengths, noise, curves):
    epoch_index = lax.broadcasted_iota(jnp.int32, (BLOCK, EPOCHS), 1)
    mask = (epoch_index < lengths[:, None]).astype(F32)
    row, col = lax.axis_index("row"), lax.axis_index("col")
    colour = lax.rem(row // NZ + 2 * lax.rem(row, NZ), 4)
    place = jnp.stack([colour, col // 2, lax.rem(col, 2)]).astype(jnp.int32)
    k_high, k_low = split(kernel_configs.reshape(-1, kernel_configs.shape[2]))

    def apply(field):
        parts = gather_row(field * mask)
        summed = scatter_col(*product(place, parts, k_high, k_low))
        smoothed = jnp.dot(summed, epoch_kernel, precision=lax.Precision.HIGHEST, preferred_element_type=F32)
        return mask * smoothed + noise[:, None] * field

    r0 = curves * mask
    w1 = apply(r0)
    w2 = apply(w1)
    rr, rw, ww, wv = reduce_all([jnp.sum(r0 * r0), jnp.sum(r0 * w1), jnp.sum(w1 * w1), jnp.sum(w1 * w2)])
    a0 = rr / rw
    rr1 = rr - 2.0 * a0 * rw + a0 * a0 * ww
    b0 = rr1 / rr
    c0 = 1.0 + b0
    curvature = c0 * c0 * rw - 2.0 * a0 * c0 * ww + a0 * a0 * wv
    a1 = rr1 / curvature
    r1 = r0 - a0 * w1
    p1 = r1 + b0 * r0
    return a0 * r0 + a1 * p1, r1 - a1 * (c0 * w1 - a0 * w2)


def solution(mesh):
    in_specs = (
        P(None, "row", "col"),
        P(),
        P(("col", "row")),
        P(("col", "row")),
        P(("col", "row"), None),
    )
    out_specs = (P(("col", "row"), None), P(("col", "row"), None))
    return jax.shard_map(
        per_device, mesh=mesh, in_specs=in_specs, out_specs=out_specs, check_vma=False
    )
```

```python
import functools

import jax
import jax.numpy as jnp
from jax import lax
from jax.experimental import pallas as pl
from jax.experimental.pallas import tpu as pltpu
from jax.sharding import PartitionSpec as P

NY, NZ, NX = 4, 8, 4
BLOCK = 64
EPOCHS = 256
F32 = jnp.float32
BF16 = jnp.bfloat16


def class_member(k, j):
    kh, kl, jh, jl = k // 2, k % 2, j // 4, j % 4
    return (kl + 2 * jh) * NZ + 2 * jl + (kh + jh) % 2


CLASSES = [[class_member(k, j) for j in range(8)] for k in range(4)]


def shift_y(d):
    return [(y * NZ + z, ((y + d) % NY) * NZ + z) for y in range(NY) for z in range(NZ)]


def shift_z(d):
    return [(y * NZ + z, y * NZ + (z + d) % NZ) for y in range(NY) for z in range(NZ)]


def shift_x(d):
    return [(x * 2 + c, ((x + d) % NX) * 2 + c) for x in range(NX) for c in range(2)]


SIBLING = [(c, c ^ 1) for c in range(8)]


def split(value):
    high = lax.reduce_precision(value, 8, 7)
    return high.astype(BF16), (value - high).astype(BF16)


def gather_class(copies):
    return lax.all_to_all(copies, "row", 0, 0, axis_index_groups=CLASSES)


def gather_rest(own):
    next_y = lax.ppermute(own, "row", shift_y(-1))
    last_y = lax.ppermute(own, "row", shift_y(1))
    next_z = lax.ppermute(own[:4], "row", shift_z(-1))
    last_z = lax.ppermute(own[4:], "row", shift_z(1))
    return own, next_y, next_z, last_z, last_y


def put_parts(colour, parts, high, low):
    for ref, slot, first in zip(parts, (0, 1, 2, 2, 3), (0, 0, 0, 4, 0)):
        k = lax.rem(colour + slot, 4)
        kh, kl = k // 2, lax.rem(k, 2)
        for j in range(ref.shape[0]):
            jh, jl = (j + first) // 4, (j + first) % 4
            row = (kl + 2 * jh) * NZ + 2 * jl + lax.rem(kh + jh, 2)
            at = pl.ds(pl.multiple_of(row * BLOCK, BLOCK), BLOCK)
            value = ref[j]
            top = value.astype(BF16)
            high[at, :] = top
            low[at, :] = (value - top.astype(F32)).astype(BF16)


def product_kernel(with_sums, place, *refs):
    parts, (k_high, k_low), refs = refs[:5], refs[5:7], refs[7:]
    if with_sums:
        images, sums, refs = refs[:4], refs[4], refs[5:]
    keep, send, high, low = refs
    put_parts(place[0], parts, high, low)
    x, even_core = place[1], place[2] == 0
    value = jnp.dot(k_high[...], high[...], preferred_element_type=F32)
    value += jnp.dot(k_low[...], high[...], preferred_element_type=F32)
    value += jnp.dot(k_high[...], low[...], preferred_element_type=F32)
    for p in range(NX):
        even = value[2 * p * BLOCK : (2 * p + 1) * BLOCK]
        odd = value[(2 * p + 1) * BLOCK : (2 * p + 2) * BLOCK]
        dx = lax.rem(p - x + NX, NX)
        keep[dx, :BLOCK] = jnp.where(even_core, even, odd)
        send[dx, :BLOCK] = jnp.where(even_core, odd, even)
    if with_sums:
        form = jnp.zeros((BLOCK, EPOCHS), F32)
        for d in range(NX):
            form += keep[d, :BLOCK] * images[d][0] + send[d, :BLOCK] * images[d][1]
        lane = lax.broadcasted_iota(jnp.int32, (8, EPOCHS), 1)
        row = lax.broadcasted_iota(jnp.int32, (8, EPOCHS), 0)
        tile = sums[...] + jnp.where((lane == 3) & (row == 0), jnp.sum(form), 0.0)
        for d in range(NX):
            keep[d, BLOCK:] = tile
            send[d, BLOCK:] = tile


VMEM_SPEC = pl.BlockSpec(memory_space=pltpu.VMEM)


def product(place, parts, k_high, k_low, extra=()):
    half = jax.ShapeDtypeStruct((NX, BLOCK + (8 if extra else 0), EPOCHS), F32)
    return pl.pallas_call(
        functools.partial(product_kernel, bool(extra)),
        out_shape=(half, half),
        in_specs=[pl.BlockSpec(memory_space=pltpu.SMEM)] + [VMEM_SPEC] * (7 + len(extra)),
        out_specs=(VMEM_SPEC, VMEM_SPEC),
        scratch_shapes=[pltpu.VMEM((2048, EPOCHS), BF16), pltpu.VMEM((2048, EPOCHS), BF16)],
        compiler_params=pltpu.CompilerParams(vmem_limit_bytes=24 * 1024 * 1024),
        cost_estimate=pl.CostEstimate(
            flops=2 * 3 * 512 * 2048 * EPOCHS, bytes_accessed=7 * 1024 * 1024, transcendentals=0
        ),
    )(place, *parts, k_high, k_low, *extra)


def dot(a, b):
    return jnp.dot(a, b, precision=lax.Precision.HIGHEST, preferred_element_type=F32)


def small_call(kernel, outs, *args):
    return pl.pallas_call(
        kernel,
        out_shape=[jax.ShapeDtypeStruct(o, F32) for o in outs],
        in_specs=[VMEM_SPEC] * len(args),
        out_specs=[VMEM_SPEC] * len(outs),
        compiler_params=pltpu.CompilerParams(vmem_limit_bytes=8 * 1024 * 1024),
        cost_estimate=pl.CostEstimate(
            flops=2 * 6 * BLOCK * EPOCHS * EPOCHS, bytes_accessed=1024 * 1024, transcendentals=0
        ),
    )(*args)


def tile_of(values, shape):
    lane = lax.broadcasted_iota(jnp.int32, shape, 1)
    row = lax.broadcasted_iota(jnp.int32, shape, 0)
    tile = jnp.zeros(shape, F32)
    for i, v in enumerate(values):
        tile = jnp.where((lane == i) & (row == 0), v, tile)
    return tile


def first_kernel(t0, t1, t2, t3, kernel, mask, noise, r0, w1, copies, image, sums):
    smoothed = dot(t0[...] + t1[...] + t2[...] + t3[...], kernel[...])
    start = r0[...]
    value = mask[...] * smoothed + noise[...] * start
    w1[...] = value
    masked = mask[...] * value
    for j in range(8):
        copies[j] = masked
    image[...] = lax.dot_general(
        masked, kernel[...], (((1,), (1,)), ((), ())),
        precision=lax.Precision.HIGHEST, preferred_element_type=F32,
    )
    sums[...] = tile_of(
        [
            jnp.sum(start * start),
            jnp.sum(start * value),
            jnp.sum(value * value),
            jnp.sum(noise[...] * value * value),
        ],
        (8, EPOCHS),
    )


def second_kernel(t0, t1, t2, t3, kernel, mask, noise, w1, w2, copies):
    total = t0[...] + t1[...] + t2[...] + t3[...]
    for j in range(32):
        copies[j] = total[BLOCK:, :128]
    w2[...] = mask[...] * dot(total[:BLOCK], kernel[...]) + noise[...] * w1[...]


def last_kernel(tiles, r0, w1, w2, out, residual):
    tile = jnp.sum(tiles[...], axis=0)
    lane = lax.broadcasted_iota(jnp.int32, (8, 128), 1)

    def pick(i):
        return jnp.sum(jnp.where(lane == i, tile, 0.0), keepdims=True)

    rr, rw, ww, wv = pick(0), pick(1), pick(2), pick(3)
    a0 = rr / rw
    rr1 = rr - 2.0 * a0 * rw + a0 * a0 * ww
    b0 = rr1 / rr
    c0 = 1.0 + b0
    a1 = rr1 / (c0 * c0 * rw - 2.0 * a0 * c0 * ww + a0 * a0 * wv)
    r1 = r0[...] - a0 * w1[...]
    out[...] = a0 * r0[...] + a1 * (r1 + b0 * r0[...])
    residual[...] = r1 - a1 * (c0 * w1[...] - a0 * w2[...])


def scatter_col(keep, send):
    other = lax.ppermute(send, "col", SIBLING)
    total = [keep[d] + other[d] for d in range(NX)]
    return total[0], *[lax.ppermute(total[d], "col", shift_x(d)) for d in range(1, NX)]


def gather_col(image):
    pair = jnp.stack([image, lax.ppermute(image, "col", SIBLING)])
    return pair, *[lax.ppermute(pair, "col", shift_x(-d)) for d in range(1, NX)]


def per_device(kernel_configs, epoch_kernel, lengths, noise, curves):
    epoch_index = lax.broadcasted_iota(jnp.int32, (BLOCK, EPOCHS), 1)
    mask = (epoch_index < lengths[:, None]).astype(F32)
    noise = jnp.broadcast_to(noise[:, None], (BLOCK, EPOCHS))
    row, col = lax.axis_index("row"), lax.axis_index("col")
    colour = lax.rem(row // NZ + 2 * lax.rem(row, NZ), 4)
    place = jnp.stack([colour, col // 2, lax.rem(col, 2)]).astype(jnp.int32)
    k_high, k_low = split(kernel_configs.reshape(-1, kernel_configs.shape[2]))
    block = (BLOCK, EPOCHS)

    r0 = curves * mask
    parts = gather_rest(gather_class(jnp.broadcast_to(r0[None], (8, BLOCK, EPOCHS))))
    pieces = scatter_col(*product(place, parts, k_high, k_low))
    w1, copies, image, sums = small_call(
        first_kernel, [block, (8, *block), block, (8, EPOCHS)], *pieces, epoch_kernel, mask, noise, r0
    )
    own, images = lax.optimization_barrier((gather_class(copies), gather_col(image)))
    parts = gather_rest(own)
    pieces = scatter_col(*product(place, parts, k_high, k_low, (*images, sums)))
    w2, copies = small_call(
        second_kernel, [block, (32, 8, 128)], *pieces, epoch_kernel, mask, noise, w1
    )
    tiles = lax.all_to_all(copies, "row", 0, 0)
    return tuple(small_call(last_kernel, [block, block], tiles, r0, w1, w2))


def solution(mesh):
    in_specs = (
        P(None, "row", "col"),
        P(),
        P(("col", "row")),
        P(("col", "row")),
        P(("col", "row"), None),
    )
    out_specs = (P(("col", "row"), None), P(("col", "row"), None))
    return jax.shard_map(
        per_device, mesh=mesh, in_specs=in_specs, out_specs=out_specs, check_vma=False
    )
```

```python
import functools

import jax
import jax.numpy as jnp
from jax import lax
from jax.experimental import pallas as pl
from jax.experimental.pallas import tpu as pltpu
from jax.sharding import PartitionSpec as P

NY, NZ, NX = 4, 8, 4
BLOCK = 64
EPOCHS = 256
F32 = jnp.float32
BF16 = jnp.bfloat16


def class_member(k, j):
    kh, kl, jh, jl = k // 2, k % 2, j // 4, j % 4
    return (kl + 2 * jh) * NZ + 2 * jl + (kh + jh) % 2


CLASSES = [[class_member(k, j) for j in range(8)] for k in range(4)]


def shift_y(d):
    return [(y * NZ + z, ((y + d) % NY) * NZ + z) for y in range(NY) for z in range(NZ)]


def shift_z(d):
    return [(y * NZ + z, y * NZ + (z + d) % NZ) for y in range(NY) for z in range(NZ)]


def shift_x(d):
    return [(x * 2 + c, ((x + d) % NX) * 2 + c) for x in range(NX) for c in range(2)]


SIBLING = [(c, c ^ 1) for c in range(8)]


def gather_class(copies):
    return lax.all_to_all(copies, "row", 0, 0, axis_index_groups=CLASSES)


def gather_rest(own):
    next_y = lax.ppermute(own, "row", shift_y(-1))
    last_y = lax.ppermute(own, "row", shift_y(1))
    lower, upper = small_call(halves_kernel, [(4, BLOCK, EPOCHS)] * 2, own)
    next_z = lax.ppermute(lower, "row", shift_z(-1))
    last_z = lax.ppermute(upper, "row", shift_z(1))
    return own, next_y, next_z, last_z, last_y


def put_parts(colour, parts, high, low):
    for ref, slot, first in zip(parts, (0, 1, 2, 2, 3), (0, 0, 0, 4, 0)):
        k = lax.rem(colour + slot, 4)
        kh, kl = k // 2, lax.rem(k, 2)
        for j in range(ref.shape[0]):
            jh, jl = (j + first) // 4, (j + first) % 4
            row = (kl + 2 * jh) * NZ + 2 * jl + lax.rem(kh + jh, 2)
            at = pl.ds(pl.multiple_of(row * BLOCK, BLOCK), BLOCK)
            value = ref[j]
            top = value.astype(BF16)
            high[at, :] = top
            low[at, :] = (value - top.astype(F32)).astype(BF16)


def product_kernel(with_sums, place, *refs):
    parts, (k_high, k_low), refs = refs[:5], refs[5:7], refs[7:]
    if with_sums:
        images, sums, refs = refs[:4], refs[4], refs[5:]
    keep, send, high, low = refs
    put_parts(place[0], parts, high, low)
    x, even_core = place[1], place[2] == 0
    value = jnp.dot(k_high[...], high[...], preferred_element_type=F32)
    value += jnp.dot(k_low[...], high[...], preferred_element_type=F32)
    value += jnp.dot(k_high[...], low[...], preferred_element_type=F32)
    for p in range(NX):
        even = value[2 * p * BLOCK : (2 * p + 1) * BLOCK]
        odd = value[(2 * p + 1) * BLOCK : (2 * p + 2) * BLOCK]
        dx = lax.rem(p - x + NX, NX)
        keep[dx, :BLOCK] = jnp.where(even_core, even, odd)
        send[dx, :BLOCK] = jnp.where(even_core, odd, even)
    if with_sums:
        form = jnp.zeros((BLOCK, EPOCHS), F32)
        for d in range(NX):
            form += keep[d, :BLOCK] * images[d][0] + send[d, :BLOCK] * images[d][1]
        lane = lax.broadcasted_iota(jnp.int32, (8, EPOCHS), 1)
        row = lax.broadcasted_iota(jnp.int32, (8, EPOCHS), 0)
        tile = sums[...] + jnp.where((lane == 3) & (row == 0), jnp.sum(form), 0.0)
        for d in range(NX):
            keep[d, BLOCK:] = tile
            send[d, BLOCK:] = tile


VMEM_SPEC = pl.BlockSpec(memory_space=pltpu.VMEM)


def split_kernel(tile, high, low):
    value = tile[...]
    top = value.astype(BF16)
    high[...] = top
    low[...] = (value - top.astype(F32)).astype(BF16)


def split(tile):
    half = jax.ShapeDtypeStruct(tile.shape, BF16)
    return pl.pallas_call(
        split_kernel,
        out_shape=(half, half),
        in_specs=[VMEM_SPEC],
        out_specs=(VMEM_SPEC, VMEM_SPEC),
        compiler_params=pltpu.CompilerParams(vmem_limit_bytes=16 * 1024 * 1024),
        cost_estimate=pl.CostEstimate(flops=4 * tile.size, bytes_accessed=8 * tile.size, transcendentals=0),
    )(tile)


def product(place, parts, k_high, k_low, extra=()):
    half = jax.ShapeDtypeStruct((NX, BLOCK + (8 if extra else 0), EPOCHS), F32)
    return pl.pallas_call(
        functools.partial(product_kernel, bool(extra)),
        out_shape=(half, half),
        in_specs=[pl.BlockSpec(memory_space=pltpu.SMEM)] + [VMEM_SPEC] * (7 + len(extra)),
        out_specs=(VMEM_SPEC, VMEM_SPEC),
        scratch_shapes=[pltpu.VMEM((2048, EPOCHS), BF16), pltpu.VMEM((2048, EPOCHS), BF16)],
        compiler_params=pltpu.CompilerParams(vmem_limit_bytes=16 * 1024 * 1024),
        cost_estimate=pl.CostEstimate(
            flops=2 * 3 * 512 * 2048 * EPOCHS, bytes_accessed=7 * 1024 * 1024, transcendentals=0
        ),
    )(place, *parts, k_high, k_low, *extra)


def dot(a, b):
    return jnp.dot(a, b, precision=lax.Precision.HIGHEST, preferred_element_type=F32)


def small_call(kernel, outs, *args, limit=4):
    return pl.pallas_call(
        kernel,
        out_shape=[jax.ShapeDtypeStruct(o, F32) for o in outs],
        in_specs=[VMEM_SPEC] * len(args),
        out_specs=[VMEM_SPEC] * len(outs),
        compiler_params=pltpu.CompilerParams(vmem_limit_bytes=limit * 1024 * 1024),
        cost_estimate=pl.CostEstimate(
            flops=2 * 6 * BLOCK * EPOCHS * EPOCHS, bytes_accessed=1024 * 1024, transcendentals=0
        ),
    )(*args)


def tile_of(values, shape):
    lane = lax.broadcasted_iota(jnp.int32, shape, 1)
    row = lax.broadcasted_iota(jnp.int32, shape, 0)
    tile = jnp.zeros(shape, F32)
    for i, v in enumerate(values):
        tile = jnp.where((lane == i) & (row == 0), v, tile)
    return tile


def first_kernel(t0, t1, t2, t3, kernel, mask, noise, r0, w1, copies, image, sums):
    smoothed = dot(t0[...] + t1[...] + t2[...] + t3[...], kernel[...])
    start = r0[...]
    value = mask[...] * smoothed + noise[...] * start
    w1[...] = value
    masked = mask[...] * value
    for j in range(8):
        copies[j] = masked
    image[...] = lax.dot_general(
        masked, kernel[...], (((1,), (1,)), ((), ())),
        precision=lax.Precision.HIGHEST, preferred_element_type=F32,
    )
    sums[...] = tile_of(
        [
            jnp.sum(start * start),
            jnp.sum(start * value),
            jnp.sum(value * value),
            jnp.sum(noise[...] * value * value),
        ],
        (8, EPOCHS),
    )


def second_kernel(t0, t1, t2, t3, kernel, mask, noise, w1, w2, copies):
    total = t0[...] + t1[...] + t2[...] + t3[...]
    for j in range(32):
        copies[j] = total[BLOCK : BLOCK + 1, :128]
    w2[...] = mask[...] * dot(total[:BLOCK], kernel[...]) + noise[...] * w1[...]


def last_kernel(tiles, r0, w1, w2, out, residual):
    tile = jnp.sum(tiles[...], axis=0)
    lane = lax.broadcasted_iota(jnp.int32, (1, 128), 1)

    def pick(i):
        return jnp.sum(jnp.where(lane == i, tile, 0.0), keepdims=True)

    rr, rw, ww, wv = pick(0), pick(1), pick(2), pick(3)
    a0 = rr / rw
    rr1 = rr - 2.0 * a0 * rw + a0 * a0 * ww
    b0 = rr1 / rr
    c0 = 1.0 + b0
    a1 = rr1 / (c0 * c0 * rw - 2.0 * a0 * c0 * ww + a0 * a0 * wv)
    r1 = r0[...] - a0 * w1[...]
    out[...] = a0 * r0[...] + a1 * (r1 + b0 * r0[...])
    residual[...] = r1 - a1 * (c0 * w1[...] - a0 * w2[...])


def halves_kernel(own, lower, upper):
    lower[...] = own[:4]
    upper[...] = own[4:]


def add_kernel(keep, other, *total):
    for d in range(NX):
        total[d][...] = keep[d] + other[d]


def pair_kernel(image, other, pair):
    pair[0] = image[...]
    pair[1] = other[...]


def scatter_col(keep, send):
    other = lax.ppermute(send, "col", SIBLING)
    total = small_call(add_kernel, [keep.shape[1:]] * NX, keep, other)
    return total[0], *[lax.ppermute(total[d], "col", shift_x(d)) for d in range(1, NX)]


def gather_col(image):
    other = lax.ppermute(image, "col", SIBLING)
    (pair,) = small_call(pair_kernel, [(2, BLOCK, EPOCHS)], image, other)
    return pair, *[lax.ppermute(pair, "col", shift_x(-d)) for d in range(1, NX)]


def per_device(kernel_configs, epoch_kernel, lengths, noise, curves):
    block = (BLOCK, EPOCHS)

    def mask_of(lengths):
        epoch_index = lax.broadcasted_iota(jnp.int32, block, 1)
        return (epoch_index < lengths[:, None]).astype(F32)

    row, col = lax.axis_index("row"), lax.axis_index("col")
    colour = lax.rem(row // NZ + 2 * lax.rem(row, NZ), 4)
    place = jnp.stack([colour, col // 2, lax.rem(col, 2)]).astype(jnp.int32)
    tile = kernel_configs.reshape(-1, kernel_configs.shape[2])

    r0 = curves * mask_of(lengths)
    own = gather_class(jnp.broadcast_to(r0[None], (8, BLOCK, EPOCHS)))
    own, first_tile, lengths, noise = lax.optimization_barrier((own, tile, lengths, noise))
    mask, noise = mask_of(lengths), jnp.broadcast_to(noise[:, None], block)
    parts = gather_rest(own)
    k_high, k_low = split(first_tile)
    pieces = scatter_col(*product(place, parts, k_high, k_low))
    w1, copies, image, sums = small_call(
        first_kernel, [block, (8, *block), block, (8, EPOCHS)], *pieces, epoch_kernel, mask, noise, r0
    )
    own, images, second_tile = lax.optimization_barrier((gather_class(copies), gather_col(image), tile))
    parts = gather_rest(own)
    k_high, k_low = split(second_tile)
    pieces = scatter_col(*product(place, parts, k_high, k_low, (*images, sums)))
    w2, copies = small_call(
        second_kernel, [block, (32, 1, 128)], *pieces, epoch_kernel, mask, noise, w1
    )
    tiles = lax.all_to_all(copies, "row", 0, 0)
    return tuple(small_call(last_kernel, [block, block], tiles, r0, w1, w2))


def solution(mesh):
    in_specs = (
        P(None, "row", "col"),
        P(),
        P(("col", "row")),
        P(("col", "row")),
        P(("col", "row"), None),
    )
    out_specs = (P(("col", "row"), None), P(("col", "row"), None))
    return jax.shard_map(
        per_device, mesh=mesh, in_specs=in_specs, out_specs=out_specs, check_vma=False
    )
```

```python
import functools

import jax
import jax.numpy as jnp
from jax import lax
from jax.experimental import pallas as pl
from jax.experimental.pallas import tpu as pltpu
from jax.sharding import PartitionSpec as P

NY, NZ, NX = 4, 8, 4
BLOCK = 64
EPOCHS = 256
F32 = jnp.float32
BF16 = jnp.bfloat16


def class_member(core, k, j):
    if core == 0:
        return (k + 2 * j) % 4 * NZ + j
    return j // 2 * NZ + (k + 2 * (j // 2)) % 4 + 4 * (j % 2)


CLASSES = [
    [class_member(col % 2, k, j) * 8 + col for j in range(8)] for col in range(8) for k in range(4)
]


def shift(major, minor):
    pairs = []
    for row in range(NY * NZ):
        for col in range(8):
            dy, dz = (major, minor) if col % 2 == 0 else (minor, major)
            target = (row // NZ + dy) % NY * NZ + (row % NZ + dz) % NZ
            pairs.append((row * 8 + col, target * 8 + col))
    return pairs


def shift_x(d):
    return [(x * 2 + c, ((x + d) % NX) * 2 + c) for x in range(NX) for c in range(2)]


SIBLING = [(c, c ^ 1) for c in range(8)]


BOTH = ("row", "col")


def gather_class(copies):
    return lax.all_to_all(copies, BOTH, 0, 0, axis_index_groups=CLASSES)


def gather_rest(own):
    above = lax.ppermute(own, BOTH, shift(-1, 0))
    below = lax.ppermute(own, BOTH, shift(1, 0))
    lower, upper = small_call(halves_kernel, [(4, BLOCK, EPOCHS)] * 2, own)
    right = lax.ppermute(lower, BOTH, shift(0, -1))
    left = lax.ppermute(upper, BOTH, shift(0, 1))
    return own, above, right, left, below


def put_parts(colour, first_core, parts, high, low):
    for ref, slot, first in zip(parts, (0, 1, 2, 2, 3), (0, 0, 0, 4, 0)):
        k = lax.rem(colour + slot, 4)
        for j in range(ref.shape[0]):
            m = j + first
            row = jnp.where(
                first_core,
                lax.rem(k + 2 * m, 4) * NZ + m,
                m // 2 * NZ + lax.rem(k + 2 * (m // 2), 4) + 4 * (m % 2),
            )
            at = pl.ds(pl.multiple_of(row * BLOCK, BLOCK), BLOCK)
            value = ref[j]
            top = value.astype(BF16)
            high[at, :] = top
            low[at, :] = (value - top.astype(F32)).astype(BF16)


def product_kernel(with_sums, place, *refs):
    parts, (k_high, k_low), refs = refs[:5], refs[5:7], refs[7:]
    if with_sums:
        images, sums, refs = refs[:4], refs[4], refs[5:]
    keep, send, high, low = refs
    x, even_core = place[1], place[2] == 0
    put_parts(place[0], even_core, parts, high, low)
    value = jnp.dot(k_high[...], high[...], preferred_element_type=F32)
    value += jnp.dot(k_low[...], high[...], preferred_element_type=F32)
    value += jnp.dot(k_high[...], low[...], preferred_element_type=F32)
    for p in range(NX):
        even = value[2 * p * BLOCK : (2 * p + 1) * BLOCK]
        odd = value[(2 * p + 1) * BLOCK : (2 * p + 2) * BLOCK]
        dx = lax.rem(p - x + NX, NX)
        keep[dx, :BLOCK] = jnp.where(even_core, even, odd)
        send[dx, :BLOCK] = jnp.where(even_core, odd, even)
    if with_sums:
        form = jnp.zeros((BLOCK, EPOCHS), F32)
        for d in range(NX):
            form += keep[d, :BLOCK] * images[d][0] + send[d, :BLOCK] * images[d][1]
        lane = lax.broadcasted_iota(jnp.int32, (8, EPOCHS), 1)
        row = lax.broadcasted_iota(jnp.int32, (8, EPOCHS), 0)
        tile = sums[...] + jnp.where((lane == 3) & (row == 0), jnp.sum(form), 0.0)
        for d in range(NX):
            keep[d, BLOCK:] = tile
            send[d, BLOCK:] = tile


VMEM_SPEC = pl.BlockSpec(memory_space=pltpu.VMEM)


def split_kernel(tile, high, low):
    value = tile[...]
    top = value.astype(BF16)
    high[...] = top
    low[...] = (value - top.astype(F32)).astype(BF16)


def split(tile):
    half = jax.ShapeDtypeStruct(tile.shape, BF16)
    return pl.pallas_call(
        split_kernel,
        out_shape=(half, half),
        in_specs=[VMEM_SPEC],
        out_specs=(VMEM_SPEC, VMEM_SPEC),
        compiler_params=pltpu.CompilerParams(vmem_limit_bytes=16 * 1024 * 1024),
        cost_estimate=pl.CostEstimate(flops=4 * tile.size, bytes_accessed=8 * tile.size, transcendentals=0),
    )(tile)


def product(place, parts, k_high, k_low, extra=()):
    half = jax.ShapeDtypeStruct((NX, BLOCK + (8 if extra else 0), EPOCHS), F32)
    return pl.pallas_call(
        functools.partial(product_kernel, bool(extra)),
        out_shape=(half, half),
        in_specs=[pl.BlockSpec(memory_space=pltpu.SMEM)] + [VMEM_SPEC] * (7 + len(extra)),
        out_specs=(VMEM_SPEC, VMEM_SPEC),
        scratch_shapes=[pltpu.VMEM((2048, EPOCHS), BF16), pltpu.VMEM((2048, EPOCHS), BF16)],
        compiler_params=pltpu.CompilerParams(vmem_limit_bytes=16 * 1024 * 1024),
        cost_estimate=pl.CostEstimate(
            flops=2 * 3 * 512 * 2048 * EPOCHS, bytes_accessed=7 * 1024 * 1024, transcendentals=0
        ),
    )(place, *parts, k_high, k_low, *extra)


def dot(a, b):
    return jnp.dot(a, b, precision=lax.Precision.HIGHEST, preferred_element_type=F32)


def small_call(kernel, outs, *args, limit=4):
    return pl.pallas_call(
        kernel,
        out_shape=[jax.ShapeDtypeStruct(o, F32) for o in outs],
        in_specs=[VMEM_SPEC] * len(args),
        out_specs=[VMEM_SPEC] * len(outs),
        compiler_params=pltpu.CompilerParams(vmem_limit_bytes=limit * 1024 * 1024),
        cost_estimate=pl.CostEstimate(
            flops=2 * 6 * BLOCK * EPOCHS * EPOCHS, bytes_accessed=1024 * 1024, transcendentals=0
        ),
    )(*args)


def tile_of(values, shape):
    lane = lax.broadcasted_iota(jnp.int32, shape, 1)
    row = lax.broadcasted_iota(jnp.int32, shape, 0)
    tile = jnp.zeros(shape, F32)
    for i, v in enumerate(values):
        tile = jnp.where((lane == i) & (row == 0), v, tile)
    return tile


def first_kernel(t0, t1, t2, t3, kernel, mask, noise, r0, w1, copies, image, sums):
    smoothed = dot(t0[...] + t1[...] + t2[...] + t3[...], kernel[...])
    start = r0[...]
    value = mask[...] * smoothed + noise[...] * start
    w1[...] = value
    masked = mask[...] * value
    for j in range(8):
        copies[j] = masked
    image[...] = lax.dot_general(
        masked, kernel[...], (((1,), (1,)), ((), ())),
        precision=lax.Precision.HIGHEST, preferred_element_type=F32,
    )
    sums[...] = tile_of(
        [
            jnp.sum(start * start),
            jnp.sum(start * value),
            jnp.sum(value * value),
            jnp.sum(noise[...] * value * value),
        ],
        (8, EPOCHS),
    )


def second_kernel(t0, t1, t2, t3, kernel, mask, noise, w1, w2, copies):
    total = t0[...] + t1[...] + t2[...] + t3[...]
    for j in range(32):
        copies[j] = total[BLOCK : BLOCK + 1, :128]
    w2[...] = mask[...] * dot(total[:BLOCK], kernel[...]) + noise[...] * w1[...]


def last_kernel(tiles, r0, w1, w2, out, residual):
    tile = jnp.sum(tiles[...], axis=0)
    lane = lax.broadcasted_iota(jnp.int32, (1, 128), 1)

    def pick(i):
        return jnp.sum(jnp.where(lane == i, tile, 0.0), keepdims=True)

    rr, rw, ww, wv = pick(0), pick(1), pick(2), pick(3)
    a0 = rr / rw
    rr1 = rr - 2.0 * a0 * rw + a0 * a0 * ww
    b0 = rr1 / rr
    c0 = 1.0 + b0
    a1 = rr1 / (c0 * c0 * rw - 2.0 * a0 * c0 * ww + a0 * a0 * wv)
    r1 = r0[...] - a0 * w1[...]
    out[...] = a0 * r0[...] + a1 * (r1 + b0 * r0[...])
    residual[...] = r1 - a1 * (c0 * w1[...] - a0 * w2[...])


def halves_kernel(own, lower, upper):
    lower[...] = own[:4]
    upper[...] = own[4:]


def add_kernel(keep, other, *total):
    for d in range(NX):
        total[d][...] = keep[d] + other[d]


def pair_kernel(image, other, pair):
    pair[0] = image[...]
    pair[1] = other[...]


def scatter_col(keep, send):
    other = lax.ppermute(send, "col", SIBLING)
    total = small_call(add_kernel, [keep.shape[1:]] * NX, keep, other)
    return total[0], *[lax.ppermute(total[d], "col", shift_x(d)) for d in range(1, NX)]


def gather_col(image):
    other = lax.ppermute(image, "col", SIBLING)
    (pair,) = small_call(pair_kernel, [(2, BLOCK, EPOCHS)], image, other)
    return pair, *[lax.ppermute(pair, "col", shift_x(-d)) for d in range(1, NX)]


def per_device(kernel_configs, epoch_kernel, lengths, noise, curves):
    block = (BLOCK, EPOCHS)

    def mask_of(lengths):
        epoch_index = lax.broadcasted_iota(jnp.int32, block, 1)
        return (epoch_index < lengths[:, None]).astype(F32)

    row, col = lax.axis_index("row"), lax.axis_index("col")
    y, z, core = row // NZ, lax.rem(row, NZ), lax.rem(col, 2)
    colour = lax.rem(jnp.where(core == 0, y + 2 * z, z + 2 * y), 4)
    place = jnp.stack([colour, col // 2, core]).astype(jnp.int32)
    tile = kernel_configs.reshape(-1, kernel_configs.shape[2])

    r0 = curves * mask_of(lengths)
    own = gather_class(jnp.broadcast_to(r0[None], (8, BLOCK, EPOCHS)))
    own, first_tile, lengths, noise = lax.optimization_barrier((own, tile, lengths, noise))
    mask, noise = mask_of(lengths), jnp.broadcast_to(noise[:, None], block)
    parts = gather_rest(own)
    k_high, k_low = split(first_tile)
    pieces = scatter_col(*product(place, parts, k_high, k_low))
    w1, copies, image, sums = small_call(
        first_kernel, [block, (8, *block), block, (8, EPOCHS)], *pieces, epoch_kernel, mask, noise, r0
    )
    own, images, second_tile = lax.optimization_barrier((gather_class(copies), gather_col(image), tile))
    parts = gather_rest(own)
    k_high, k_low = split(second_tile)
    pieces = scatter_col(*product(place, parts, k_high, k_low, (*images, sums)))
    w2, copies = small_call(
        second_kernel, [block, (32, 1, 128)], *pieces, epoch_kernel, mask, noise, w1
    )
    tiles = lax.all_to_all(copies, "row", 0, 0)
    return tuple(small_call(last_kernel, [block, block], tiles, r0, w1, w2))


def solution(mesh):
    in_specs = (
        P(None, "row", "col"),
        P(),
        P(("col", "row")),
        P(("col", "row")),
        P(("col", "row"), None),
    )
    out_specs = (P(("col", "row"), None), P(("col", "row"), None))
    return jax.shard_map(
        per_device, mesh=mesh, in_specs=in_specs, out_specs=out_specs, check_vma=False
    )
```

```python
import functools

import jax
import jax.numpy as jnp
from jax import lax
from jax.experimental import pallas as pl
from jax.experimental.pallas import tpu as pltpu
from jax.sharding import PartitionSpec as P

NY, NZ, NX = 4, 8, 4
BLOCK = 64
EPOCHS = 256
F32 = jnp.float32
BF16 = jnp.bfloat16


def class_member(core, k, j):
    if core == 0:
        return (k + 2 * j) % 4 * NZ + j
    return j // 2 * NZ + (k + 2 * (j // 2)) % 4 + 4 * (j % 2)


CLASSES = [
    [class_member(col % 2, k, j) * 8 + col for j in range(8)] for col in range(8) for k in range(4)
]


def shift(major, minor):
    pairs = []
    for row in range(NY * NZ):
        for col in range(8):
            dy, dz = (major, minor) if col % 2 == 0 else (minor, major)
            target = (row // NZ + dy) % NY * NZ + (row % NZ + dz) % NZ
            pairs.append((row * 8 + col, target * 8 + col))
    return pairs


def shift_x(d):
    return [(x * 2 + c, ((x + d) % NX) * 2 + c) for x in range(NX) for c in range(2)]


SIBLING = [(c, c ^ 1) for c in range(8)]


BOTH = ("row", "col")


def gather_class(copies):
    return lax.all_to_all(copies, BOTH, 0, 0, axis_index_groups=CLASSES)


def gather_rest(own):
    above = lax.ppermute(own, BOTH, shift(-1, 0))
    below = lax.ppermute(own, BOTH, shift(1, 0))
    lower, upper = small_call(halves_kernel, [(4, BLOCK, EPOCHS)] * 2, own)
    right = lax.ppermute(lower, BOTH, shift(0, -1))
    left = lax.ppermute(upper, BOTH, shift(0, 1))
    return own, above, right, left, below


def put_parts(place, parts, high, low):
    colour, first_core = place[0], place[2] == 0
    for ref, slot, first in zip(parts, (0, 1, 2, 2, 3), (0, 0, 0, 4, 0)):
        k = (colour + slot) & 3
        shifts = (k, (k + 2) & 3)
        for j in range(ref.shape[0]):
            m = j + first
            row = jnp.where(
                first_core, shifts[m % 2] * NZ + m, shifts[m // 2 % 2] + (m // 2 * NZ + 4 * (m % 2))
            )
            at = pl.ds(pl.multiple_of(row * BLOCK, BLOCK), BLOCK)
            value = ref[j]
            top = value.astype(BF16)
            high[at, :] = top
            low[at, :] = (value - top.astype(F32)).astype(BF16)


def multiply(k_high, k_low, half, high, low):
    top = k_high[half].reshape(NX * BLOCK, -1)
    value = jnp.dot(top, high[...], preferred_element_type=F32)
    value += jnp.dot(k_low[half].reshape(NX * BLOCK, -1), high[...], preferred_element_type=F32)
    value += jnp.dot(top, low[...], preferred_element_type=F32)
    return value.reshape(NX, BLOCK, EPOCHS)


KEEP, SEND = 0, 1


def send_kernel(place, own, above, right, left, below, k_high, k_low, send, high, low):
    put_parts(place, (own, above, right, left, below), high, low)
    send[...] = multiply(k_high, k_low, SEND, high, low)


def keep_kernel(k_high, k_low, high, low, keep):
    keep[...] = multiply(k_high, k_low, KEEP, high, low)


def both_kernel(place, own, above, right, left, below, k_high, k_low, *refs):
    images, (sums, keep, send, high, low) = refs[:4], refs[4:]
    put_parts(place, (own, above, right, left, below), high, low)
    form = jnp.zeros((BLOCK, EPOCHS), F32)
    for half, out in ((SEND, send), (KEEP, keep)):
        value = multiply(k_high, k_low, half, high, low)
        for d in range(NX):
            out[d, :BLOCK] = value[d]
            form += value[d] * images[d][half]
    lane = lax.broadcasted_iota(jnp.int32, (8, EPOCHS), 1)
    row = lax.broadcasted_iota(jnp.int32, (8, EPOCHS), 0)
    tile = sums[...] + jnp.where((lane == 3) & (row == 0), jnp.sum(form), 0.0)
    for d in range(NX):
        keep[d, BLOCK:] = tile
        send[d, BLOCK:] = tile


VMEM_SPEC = pl.BlockSpec(memory_space=pltpu.VMEM)


SMEM_SPEC = pl.BlockSpec(memory_space=pltpu.SMEM)


def split_kernel(place, tile, high, low):
    x, core = place[1], place[2]
    for b in range(2 * NX):
        half, dx = (core + b) & 1, (b // 2 - x) & 3
        value = tile[b]
        top = value.astype(BF16)
        high[half, dx] = top
        low[half, dx] = (value - top.astype(F32)).astype(BF16)


def large_call(kernel, outs, in_specs, flops, scratch=()):
    return pl.pallas_call(
        kernel,
        out_shape=[jax.ShapeDtypeStruct(*o) for o in outs],
        in_specs=in_specs,
        out_specs=[VMEM_SPEC] * len(outs),
        scratch_shapes=scratch,
        compiler_params=pltpu.CompilerParams(vmem_limit_bytes=16 * 1024 * 1024),
        cost_estimate=pl.CostEstimate(flops=flops, bytes_accessed=7 * 1024 * 1024, transcendentals=0),
    )


def split(place, tile):
    out = ((2, NX, BLOCK, tile.shape[2]), BF16)
    return large_call(split_kernel, [out, out], [SMEM_SPEC, VMEM_SPEC], 4 * tile.size)(place, tile)


PRODUCT_FLOPS = 2 * 3 * 512 * 2048 * EPOCHS
FIELD = (2048, EPOCHS)


def first_product(place, parts, k_high, k_low):
    half = ((NX, BLOCK, EPOCHS), F32)
    send, high, low = large_call(
        send_kernel,
        [half, (FIELD, BF16), (FIELD, BF16)],
        [SMEM_SPEC] + [VMEM_SPEC] * 7,
        PRODUCT_FLOPS // 2,
    )(place, *parts, k_high, k_low)
    (keep,) = large_call(keep_kernel, [half], [VMEM_SPEC] * 4, PRODUCT_FLOPS // 2)(k_high, k_low, high, low)
    return keep, send


def second_product(place, parts, k_high, k_low, images, sums):
    half = ((NX, BLOCK + 8, EPOCHS), F32)
    return large_call(
        both_kernel,
        [half, half],
        [SMEM_SPEC] + [VMEM_SPEC] * 12,
        PRODUCT_FLOPS,
        [pltpu.VMEM(FIELD, BF16), pltpu.VMEM(FIELD, BF16)],
    )(place, *parts, k_high, k_low, *images, sums)


def dot(a, b):
    return jnp.dot(a, b, precision=lax.Precision.HIGHEST, preferred_element_type=F32)


def small_call(kernel, outs, *args, limit=4):
    return pl.pallas_call(
        kernel,
        out_shape=[jax.ShapeDtypeStruct(o, F32) for o in outs],
        in_specs=[VMEM_SPEC] * len(args),
        out_specs=[VMEM_SPEC] * len(outs),
        compiler_params=pltpu.CompilerParams(vmem_limit_bytes=limit * 1024 * 1024),
        cost_estimate=pl.CostEstimate(
            flops=2 * 6 * BLOCK * EPOCHS * EPOCHS, bytes_accessed=1024 * 1024, transcendentals=0
        ),
    )(*args)


def tile_of(values, shape):
    lane = lax.broadcasted_iota(jnp.int32, shape, 1)
    row = lax.broadcasted_iota(jnp.int32, shape, 0)
    tile = jnp.zeros(shape, F32)
    for i, v in enumerate(values):
        tile = jnp.where((lane == i) & (row == 0), v, tile)
    return tile


def first_kernel(t0, t1, t2, t3, kernel, mask, noise, r0, w1, copies, image, sums):
    smoothed = dot(t0[...] + t1[...] + t2[...] + t3[...], kernel[...])
    start = r0[...]
    value = mask[...] * smoothed + noise[...] * start
    w1[...] = value
    masked = mask[...] * value
    for j in range(8):
        copies[j] = masked
    image[...] = lax.dot_general(
        masked, kernel[...], (((1,), (1,)), ((), ())),
        precision=lax.Precision.HIGHEST, preferred_element_type=F32,
    )
    sums[...] = tile_of(
        [
            jnp.sum(start * start),
            jnp.sum(start * value),
            jnp.sum(value * value),
            jnp.sum(noise[...] * value * value),
        ],
        (8, EPOCHS),
    )


def second_kernel(t0, t1, t2, t3, kernel, mask, noise, w1, w2, copies):
    total = t0[...] + t1[...] + t2[...] + t3[...]
    for j in range(32):
        copies[j] = total[BLOCK : BLOCK + 1, :128]
    w2[...] = mask[...] * dot(total[:BLOCK], kernel[...]) + noise[...] * w1[...]


def last_kernel(tiles, r0, w1, w2, out, residual):
    tile = jnp.sum(tiles[...], axis=0)
    lane = lax.broadcasted_iota(jnp.int32, (1, 128), 1)

    def pick(i):
        return jnp.sum(jnp.where(lane == i, tile, 0.0), keepdims=True)

    rr, rw, ww, wv = pick(0), pick(1), pick(2), pick(3)
    a0 = rr / rw
    rr1 = rr - 2.0 * a0 * rw + a0 * a0 * ww
    b0 = rr1 / rr
    c0 = 1.0 + b0
    a1 = rr1 / (c0 * c0 * rw - 2.0 * a0 * c0 * ww + a0 * a0 * wv)
    r1 = r0[...] - a0 * w1[...]
    out[...] = a0 * r0[...] + a1 * (r1 + b0 * r0[...])
    residual[...] = r1 - a1 * (c0 * w1[...] - a0 * w2[...])


def halves_kernel(own, lower, upper):
    lower[...] = own[:4]
    upper[...] = own[4:]


def add_kernel(keep, other, *total):
    for d in range(NX):
        total[d][...] = keep[d] + other[d]


def pair_kernel(image, other, pair):
    pair[0] = image[...]
    pair[1] = other[...]


def scatter_col(keep, send):
    other = lax.ppermute(send, "col", SIBLING)
    total = small_call(add_kernel, [keep.shape[1:]] * NX, keep, other)
    return total[0], *[lax.ppermute(total[d], "col", shift_x(d)) for d in (2, 1, 3)]


def gather_col(image):
    other = lax.ppermute(image, "col", SIBLING)
    (pair,) = small_call(pair_kernel, [(2, BLOCK, EPOCHS)], image, other)
    return pair, *[lax.ppermute(pair, "col", shift_x(-d)) for d in range(1, NX)]


def per_device(kernel_configs, epoch_kernel, lengths, noise, curves):
    block = (BLOCK, EPOCHS)

    def mask_of(lengths):
        epoch_index = lax.broadcasted_iota(jnp.int32, block, 1)
        return (epoch_index < lengths[:, None]).astype(F32)

    row, col = lax.axis_index("row"), lax.axis_index("col")
    y, z, core = row // NZ, lax.rem(row, NZ), lax.rem(col, 2)
    colour = lax.rem(jnp.where(core == 0, y + 2 * z, z + 2 * y), 4)
    place = jnp.stack([colour, col // 2, core]).astype(jnp.int32)
    tile = kernel_configs

    r0 = curves * mask_of(lengths)
    own = gather_class(jnp.broadcast_to(r0[None], (8, BLOCK, EPOCHS)))
    own, first_tile, lengths, noise = lax.optimization_barrier((own, tile, lengths, noise))
    mask, noise = mask_of(lengths), jnp.broadcast_to(noise[:, None], block)
    parts = gather_rest(own)
    k_high, k_low = split(place, first_tile)
    pieces = scatter_col(*first_product(place, parts, k_high, k_low))
    w1, copies, image, sums = small_call(
        first_kernel, [block, (8, *block), block, (8, EPOCHS)], *pieces, epoch_kernel, mask, noise, r0
    )
    own, images, second_tile = lax.optimization_barrier((gather_class(copies), gather_col(image), tile))
    parts = gather_rest(own)
    k_high, k_low = split(place, second_tile)
    pieces = scatter_col(*second_product(place, parts, k_high, k_low, images, sums))
    w2, copies = small_call(
        second_kernel, [block, (32, 1, 128)], *pieces, epoch_kernel, mask, noise, w1
    )
    tiles = lax.all_to_all(copies, "row", 0, 0)
    return tuple(small_call(last_kernel, [block, block], tiles, r0, w1, w2))


def solution(mesh):
    in_specs = (
        P(None, "row", "col"),
        P(),
        P(("col", "row")),
        P(("col", "row")),
        P(("col", "row"), None),
    )
    out_specs = (P(("col", "row"), None), P(("col", "row"), None))
    return jax.shard_map(
        per_device, mesh=mesh, in_specs=in_specs, out_specs=out_specs, check_vma=False
    )
```

```python
import functools

import jax
import jax.numpy as jnp
from jax import lax
from jax.experimental import pallas as pl
from jax.experimental.pallas import tpu as pltpu
from jax.sharding import PartitionSpec as P

NY, NZ, NX = 4, 8, 4
BLOCK = 64
EPOCHS = 256
F32 = jnp.float32
BF16 = jnp.bfloat16


def class_member(core, k, j):
    if core == 0:
        return (k + 2 * j) % 4 * NZ + j
    return j // 2 * NZ + (k + 2 * (j // 2)) % 4 + 4 * (j % 2)


CLASSES = [
    [class_member(col % 2, k, j) * 8 + col for j in range(8)] for col in range(8) for k in range(4)
]


def shift(major, minor):
    pairs = []
    for row in range(NY * NZ):
        for col in range(8):
            dy, dz = (major, minor) if col % 2 == 0 else (minor, major)
            target = (row // NZ + dy) % NY * NZ + (row % NZ + dz) % NZ
            pairs.append((row * 8 + col, target * 8 + col))
    return pairs


def shift_x(d):
    return [(x * 2 + c, ((x + d) % NX) * 2 + c) for x in range(NX) for c in range(2)]


SIBLING = [(c, c ^ 1) for c in range(8)]


BOTH = ("row", "col")


def gather_class(copies):
    return lax.all_to_all(copies, BOTH, 0, 0, axis_index_groups=CLASSES)


def gather_rest(own):
    above = lax.ppermute(own, BOTH, shift(-1, 0))
    below = lax.ppermute(own, BOTH, shift(1, 0))
    lower, upper = small_call(halves_kernel, [(4, BLOCK, EPOCHS)] * 2, own)
    right = lax.ppermute(lower, BOTH, shift(0, -1))
    left = lax.ppermute(upper, BOTH, shift(0, 1))
    return own, above, right, left, below


def put_parts(place, parts, high, low):
    colour, first_core = place[0], place[2] == 0
    for ref, slot, first in zip(parts, (0, 1, 2, 2, 3), (0, 0, 0, 4, 0)):
        k = (colour + slot) & 3
        shifts = (k, (k + 2) & 3)
        for j in range(ref.shape[0]):
            m = j + first
            row = jnp.where(
                first_core, shifts[m % 2] * NZ + m, shifts[m // 2 % 2] + (m // 2 * NZ + 4 * (m % 2))
            )
            at = pl.ds(pl.multiple_of(row * BLOCK, BLOCK), BLOCK)
            value = ref[j]
            top = value.astype(BF16)
            high[at, :] = top
            low[at, :] = (value - top.astype(F32)).astype(BF16)


def multiply(k_high, k_low, half, high, low):
    top = k_high[half].reshape(NX * BLOCK, -1)
    value = jnp.dot(top, high[...], preferred_element_type=F32)
    value += jnp.dot(k_low[half].reshape(NX * BLOCK, -1), high[...], preferred_element_type=F32)
    value += jnp.dot(top, low[...], preferred_element_type=F32)
    return value.reshape(NX, BLOCK, EPOCHS)


KEEP, SEND = 0, 1


def send_kernel(place, own, above, right, left, below, k_high, k_low, send, high, low):
    put_parts(place, (own, above, right, left, below), high, low)
    send[...] = multiply(k_high, k_low, SEND, high, low)


def keep_kernel(k_high, k_low, high, low, keep):
    keep[...] = multiply(k_high, k_low, KEEP, high, low)


def both_kernel(place, own, above, right, left, below, k_high, k_low, *refs):
    images, (sums, keep, send, high, low) = refs[:4], refs[4:]
    put_parts(place, (own, above, right, left, below), high, low)
    form = jnp.zeros((BLOCK, EPOCHS), F32)
    for half, out in ((SEND, send), (KEEP, keep)):
        value = multiply(k_high, k_low, half, high, low)
        for d in range(NX):
            out[d, :BLOCK] = value[d]
            form += value[d] * images[d][half]
    lane = lax.broadcasted_iota(jnp.int32, (8, EPOCHS), 1)
    row = lax.broadcasted_iota(jnp.int32, (8, EPOCHS), 0)
    tile = sums[...] + jnp.where((lane == 3) & (row == 0), jnp.sum(form), 0.0)
    for d in range(NX):
        keep[d, BLOCK:] = tile
        send[d, BLOCK:] = tile


VMEM_SPEC = pl.BlockSpec(memory_space=pltpu.VMEM)


SMEM_SPEC = pl.BlockSpec(memory_space=pltpu.SMEM)


def split_kernel(place, tile, high, low):
    x, core = place[1], place[2]
    for b in range(2 * NX):
        half, dx = (core + b) & 1, (b // 2 - x) & 3
        value = tile[b]
        top = value.astype(BF16)
        high[half, dx] = top
        low[half, dx] = (value - top.astype(F32)).astype(BF16)


def large_call(kernel, outs, in_specs, flops, scratch=()):
    return pl.pallas_call(
        kernel,
        out_shape=[jax.ShapeDtypeStruct(*o) for o in outs],
        in_specs=in_specs,
        out_specs=[VMEM_SPEC] * len(outs),
        scratch_shapes=scratch,
        compiler_params=pltpu.CompilerParams(vmem_limit_bytes=16 * 1024 * 1024),
        cost_estimate=pl.CostEstimate(flops=flops, bytes_accessed=7 * 1024 * 1024, transcendentals=0),
    )


def split(place, tile):
    out = ((2, NX, BLOCK, tile.shape[2]), BF16)
    return large_call(split_kernel, [out, out], [SMEM_SPEC, VMEM_SPEC], 4 * tile.size)(place, tile)


PRODUCT_FLOPS = 2 * 3 * 512 * 2048 * EPOCHS
FIELD = (2048, EPOCHS)


def first_product(place, parts, k_high, k_low):
    half = ((NX, BLOCK, EPOCHS), F32)
    send, high, low = large_call(
        send_kernel,
        [half, (FIELD, BF16), (FIELD, BF16)],
        [SMEM_SPEC] + [VMEM_SPEC] * 7,
        PRODUCT_FLOPS // 2,
    )(place, *parts, k_high, k_low)
    (keep,) = large_call(keep_kernel, [half], [VMEM_SPEC] * 4, PRODUCT_FLOPS // 2)(k_high, k_low, high, low)
    return keep, send


def second_product(place, parts, k_high, k_low, images, sums):
    half = ((NX, BLOCK + 8, EPOCHS), F32)
    return large_call(
        both_kernel,
        [half, half],
        [SMEM_SPEC] + [VMEM_SPEC] * 12,
        PRODUCT_FLOPS,
        [pltpu.VMEM(FIELD, BF16), pltpu.VMEM(FIELD, BF16)],
    )(place, *parts, k_high, k_low, *images, sums)


def dot(a, b):
    return jnp.dot(a, b, precision=lax.Precision.HIGHEST, preferred_element_type=F32)


def small_call(kernel, outs, *args, limit=4):
    return pl.pallas_call(
        kernel,
        out_shape=[jax.ShapeDtypeStruct(o, F32) for o in outs],
        in_specs=[VMEM_SPEC] * len(args),
        out_specs=[VMEM_SPEC] * len(outs),
        compiler_params=pltpu.CompilerParams(vmem_limit_bytes=limit * 1024 * 1024),
        cost_estimate=pl.CostEstimate(
            flops=2 * 6 * BLOCK * EPOCHS * EPOCHS, bytes_accessed=1024 * 1024, transcendentals=0
        ),
    )(*args)


def tile_of(values, shape):
    lane = lax.broadcasted_iota(jnp.int32, shape, 1)
    row = lax.broadcasted_iota(jnp.int32, shape, 0)
    tile = jnp.zeros(shape, F32)
    for i, v in enumerate(values):
        tile = jnp.where((lane == i) & (row == 0), v, tile)
    return tile


def first_kernel(t0, t1, t2, t3, kernel, mask, noise, r0, w1, copies):
    smoothed = dot(t0[...] + t1[...] + t2[...] + t3[...], kernel[...])
    start = r0[...]
    value = mask[...] * smoothed + noise[...] * start
    w1[...] = value
    masked = mask[...] * value
    for j in range(8):
        copies[j] = masked


def image_kernel(kernel, mask, noise, r0, w1, image, sums):
    start, value = r0[...], w1[...]
    image[...] = lax.dot_general(
        mask[...] * value, kernel[...], (((1,), (1,)), ((), ())),
        precision=lax.Precision.HIGHEST, preferred_element_type=F32,
    )
    sums[...] = tile_of(
        [
            jnp.sum(start * start),
            jnp.sum(start * value),
            jnp.sum(value * value),
            jnp.sum(noise[...] * value * value),
        ],
        (8, EPOCHS),
    )


def second_kernel(t0, t1, t2, t3, kernel, mask, noise, w1, w2, copies):
    total = t0[...] + t1[...] + t2[...] + t3[...]
    for j in range(32):
        copies[j] = total[BLOCK : BLOCK + 1, :128]
    w2[...] = mask[...] * dot(total[:BLOCK], kernel[...]) + noise[...] * w1[...]


def last_kernel(tiles, r0, w1, w2, out, residual):
    tile = jnp.sum(tiles[...], axis=0)
    lane = lax.broadcasted_iota(jnp.int32, (1, 128), 1)

    def pick(i):
        return jnp.sum(jnp.where(lane == i, tile, 0.0), keepdims=True)

    rr, rw, ww, wv = pick(0), pick(1), pick(2), pick(3)
    a0 = rr / rw
    rr1 = rr - 2.0 * a0 * rw + a0 * a0 * ww
    b0 = rr1 / rr
    c0 = 1.0 + b0
    a1 = rr1 / (c0 * c0 * rw - 2.0 * a0 * c0 * ww + a0 * a0 * wv)
    r1 = r0[...] - a0 * w1[...]
    out[...] = a0 * r0[...] + a1 * (r1 + b0 * r0[...])
    residual[...] = r1 - a1 * (c0 * w1[...] - a0 * w2[...])


def halves_kernel(own, lower, upper):
    lower[...] = own[:4]
    upper[...] = own[4:]


def add_kernel(keep, other, *total):
    for d in range(NX):
        total[d][...] = keep[d] + other[d]


def pair_kernel(image, other, pair):
    pair[0] = image[...]
    pair[1] = other[...]


def scatter_col(keep, send):
    other = lax.ppermute(send, "col", SIBLING)
    total = small_call(add_kernel, [keep.shape[1:]] * NX, keep, other)
    return total[0], *[lax.ppermute(total[d], "col", shift_x(d)) for d in (2, 1, 3)]


def gather_col(image):
    other = lax.ppermute(image, "col", SIBLING)
    (pair,) = small_call(pair_kernel, [(2, BLOCK, EPOCHS)], image, other)
    return pair, *[lax.ppermute(pair, "col", shift_x(-d)) for d in range(1, NX)]


def per_device(kernel_configs, epoch_kernel, lengths, noise, curves):
    block = (BLOCK, EPOCHS)

    def mask_of(lengths):
        epoch_index = lax.broadcasted_iota(jnp.int32, block, 1)
        return (epoch_index < lengths[:, None]).astype(F32)

    row, col = lax.axis_index("row"), lax.axis_index("col")
    y, z, core = row // NZ, lax.rem(row, NZ), lax.rem(col, 2)
    colour = lax.rem(jnp.where(core == 0, y + 2 * z, z + 2 * y), 4)
    place = jnp.stack([colour, col // 2, core]).astype(jnp.int32)
    tile = kernel_configs

    r0 = curves * mask_of(lengths)
    own = gather_class(jnp.broadcast_to(r0[None], (8, BLOCK, EPOCHS)))
    own, first_tile, lengths, noise = lax.optimization_barrier((own, tile, lengths, noise))
    mask, noise = mask_of(lengths), jnp.broadcast_to(noise[:, None], block)
    parts = gather_rest(own)
    k_high, k_low = split(place, first_tile)
    pieces = scatter_col(*first_product(place, parts, k_high, k_low))
    w1, copies = small_call(
        first_kernel, [block, (8, *block)], *pieces, epoch_kernel, mask, noise, r0
    )
    image, sums = small_call(image_kernel, [block, (8, EPOCHS)], epoch_kernel, mask, noise, r0, w1)
    own, images, second_tile = lax.optimization_barrier((gather_class(copies), gather_col(image), tile))
    parts = gather_rest(own)
    k_high, k_low = split(place, second_tile)
    pieces = scatter_col(*second_product(place, parts, k_high, k_low, images, sums))
    w2, copies = small_call(
        second_kernel, [block, (32, 1, 128)], *pieces, epoch_kernel, mask, noise, w1
    )
    tiles = lax.all_to_all(copies, "row", 0, 0)
    return tuple(small_call(last_kernel, [block, block], tiles, r0, w1, w2))


def solution(mesh):
    in_specs = (
        P(None, "row", "col"),
        P(),
        P(("col", "row")),
        P(("col", "row")),
        P(("col", "row"), None),
    )
    out_specs = (P(("col", "row"), None), P(("col", "row"), None))
    return jax.shard_map(
        per_device, mesh=mesh, in_specs=in_specs, out_specs=out_specs, check_vma=False
    )
```
